128 devices in a mesh: vol: 16 (over x_hi, y, core), rate: 8 (over z, x_lo).
Axes of the slice: x: 4 (x_hi: 2, x_lo: 2; x = x_hi * 2 + x_lo), y: 4, z: 4, core: 2. Of those that a mesh axis runs over, the one named last changes fastest.
Arguments:
- value_next: float32 [256, 64, 2048], P('vol', 'rate'), may hold values from -6 to 6
- risk_cost: float32 [8, 256], P(None, 'vol'), may hold values from -4 to 4
- band_start: int32 [8, 2048], replicated, may hold values from 0 to 2046, as said below
- band_weight: float32 [8, 2048], replicated, may hold values from 0 to 1
- felicity_array: float32 [2048], replicated, may hold values from -4 to 4
Outputs:
- value_now: float32 [256, 64, 2048], P('vol', 'rate')
The draws below stay inside these ranges and needn't reach their ends.
Inputs may be any that keep to these rules, and one draw needn't show every extreme that they name: band_start[a, w] lies between w - 64 and w + 62 for every allocation a and wealth point w.
All inputs are finite; a program needn't handle non-finite values.
Results may differ from the reference program's by a relative error of at most 0.00002.
Values sent between devices are 32-bit elements; how exact they have to be, the bound alone decides.
No kernel may reach another device: no remote copies, remote signals or barrier semaphores. Data moves between devices by JAX's collectives and lax.ppermute only.
A program may use at most 320 MiB of HBM per device.

```python
import jax
import jax.numpy as jnp

ASSET_LEVELS = 2048
ALLOC = 8
SECTIONS = 2
VOL = 256
RATE = 64


def draw_band_start(key, part):
    key = jax.random.fold_in(key, 7)
    offsets = jax.random.randint(key, (ALLOC, ASSET_LEVELS), -64, 63, dtype=jnp.int32)
    places = jnp.arange(ASSET_LEVELS, dtype=jnp.int32)[None, :]
    return jnp.clip(places + offsets, 0, ASSET_LEVELS - 2).astype(jnp.int32)


def steps_of(key, extent, shards, least, top_value):
    factor_of, own = 1.0, jax.random.fold_in(key, 6)
    for dim, shards_of in shards:
        heights = jnp.exp(jax.random.uniform(jax.random.fold_in(own, dim), (shards_of,), jnp.float32, least / len(shards), top_value / len(shards)))
        factor_of = factor_of * jnp.repeat(heights, extent[dim] // shards_of).reshape([-1 if axis == dim else 1 for axis in range(len(extent))])
    return factor_of


def bell_draw(rng, extent, deviation, bound, shards=(), held_as=jnp.bfloat16):
    array = deviation * jax.random.normal(rng, extent, jnp.float32)
    if shards:
        array = array * steps_of(rng, extent, shards, -0.22, 0.18)
    return jnp.clip(array, -bound, bound).astype(held_as)


def setup_inputs(seed: int = 0) -> dict:
    seeds = jax.random.split(jax.random.key(seed), 6)
    return {
        "value_next": bell_draw(seeds[0], (VOL, RATE, ASSET_LEVELS), 1.0, 6.0, ((0, 16), (1, 8)), jnp.float32),
        "risk_cost": bell_draw(seeds[1], (ALLOC, VOL), 1.0, 4.0, ((1, 16),), jnp.float32),
        "band_start": draw_band_start(jax.random.fold_in(seeds[5], 71), 0),
        "band_weight": jnp.clip(jax.random.uniform(seeds[3], (ALLOC, ASSET_LEVELS), jnp.float32, 0.0, 1.0), 0.0, 1.0),
        "felicity_array": bell_draw(seeds[4], (ASSET_LEVELS,), 1.0, 4.0, (), jnp.float32),
    }


hermite_weights = (0.000548269, 0.030757124, 0.240123178, 0.457142857, 0.240123178, 0.030757124, 0.000548269)
discount = 0.96
smoothing_coefficient = 0.5


def smooth(field, along):
    section_length = field.shape[along]
    widths = [(0, 0)] * field.ndim
    widths[along] = (3, 3)
    padded = jnp.pad(field, widths)
    result = jnp.zeros_like(field)
    for start_shift in range(7):
        result = result + hermite_weights[start_shift] * jax.lax.slice_in_dim(padded, start_shift, start_shift + section_length, axis=along)
    return result


def settle(expected, risk_part, band_start, band_weight, felicity_array):
    normalizer_sum = jnp.zeros(expected.shape, jnp.float32)
    for option in range(band_start.shape[0]):
        lower_node = jnp.take(expected, band_start[option], axis=2)
        higher_gridpoint = jnp.take(expected, band_start[option] + 1, axis=2)
        quadrature_weight_row = band_weight[option][None, None, :]
        cont = (1.0 - quadrature_weight_row) * lower_node + quadrature_weight_row * higher_gridpoint
        candidate_logits = discount * cont - risk_part[option][:, None, None]
        normalizer_sum = normalizer_sum + jnp.exp(candidate_logits / smoothing_coefficient)
    return smoothing_coefficient * jnp.log(normalizer_sum) + felicity_array[None, None, :]


def reference(value_next, risk_cost, band_start, band_weight, felicity_array):
    ongoing_estimate = value_next
    for age_index in range(SECTIONS):
        expected = smooth(smooth(ongoing_estimate, 0), 1)
        ongoing_estimate = settle(expected, risk_cost, band_start, band_weight, felicity_array)
    return ongoing_estimate
```

```python
import functools

import jax
import jax.numpy as jnp
from jax import lax
from jax.experimental import pallas as pl
from jax.experimental.pallas import tpu as pltpu
from jax.sharding import PartitionSpec as P

GAUSS = (
    0.000548269,
    0.030757124,
    0.240123178,
    0.457142857,
    0.240123178,
    0.030757124,
    0.000548269,
)
REACH = 3
WIDE = 2 * REACH
LOG2E = 1.4426950408889634
LN2 = 0.6931471805599453
DISCOUNT = 0.96
SMOOTHING = 0.5
LANES = 128
SCALE = DISCOUNT / SMOOTHING * LOG2E

F32 = jnp.float32
BF16 = jnp.bfloat16

CHUNKS = 4
EDGE = 8
SMOOTH_COST = 10**9
SETTLE_COST = 4 * 10**9

SMEM = pl.BlockSpec(memory_space=pltpu.SMEM)
VMEM = pl.BlockSpec(memory_space=pltpu.VMEM)
VMEM_LIMIT = 24 * 2**20


def repeat(count, step, body):
    turns = count // step
    if turns > 1:

        def turn(t, carry):
            for q in range(step):
                body(t * step + q)
            return carry

        lax.fori_loop(0, turns, turn, 0)
        done = turns * step
    else:
        done = 0
    for q in range(done, count):
        body(q)


def lanes_of(tile, count=1):
    if isinstance(tile, int):
        return pl.ds(tile * LANES, count * LANES)
    return pl.ds(pl.multiple_of(tile * LANES, LANES), count * LANES)


def cost(flops):
    return pl.CostEstimate(flops=flops, bytes_accessed=0, transcendentals=0)


def smooth_rows(layers):
    rows = []
    for i in range(len(layers) - WIDE):
        total = GAUSS[REACH] * layers[i + REACH]
        for j in range(REACH):
            total = total + GAUSS[j] * (layers[i + j] + layers[i + WIDE - j])
        rows.append(total)
    return rows


def inner_kernel(own, sent, kept):
    def body(tile):
        at = lanes_of(tile)
        first = EDGE // 2
        layers = [own[i, :, at] for i in range(first - REACH, own.shape[0] - first + REACH)]
        turned = jnp.swapaxes(jnp.stack(smooth_rows(layers)), 0, 1)
        sent[:, :, at] = turned[:WIDE]
        kept[:, :, at] = turned[WIDE:]

    repeat(own.shape[-1] // LANES, 2, body)


def outer_kernel(side, own, near, far, sent, kept):
    first_core = side[0] != 0

    def body(tile):
        at = lanes_of(tile)
        pairs = [(near[i, :, at], far[i, :, at]) for i in range(WIDE)]
        low = [jnp.where(first_core, f, n) for n, f in pairs]
        high = [jnp.where(first_core, n, f) for n, f in pairs]
        count = own.shape[0]
        half = EDGE // 2
        low += [own[i, :, at] for i in range(half + REACH)]
        high = [own[i, :, at] for i in range(count - half - REACH, count)] + high
        nothing = jnp.zeros_like(low[0])
        rows = [nothing] + smooth_rows(low) + smooth_rows(high) + [nothing]
        turned = jnp.swapaxes(jnp.stack(rows), 0, 1)
        sent[:, :, at] = turned[:WIDE]
        kept[:, :, at] = turned[WIDE:]

    repeat(own.shape[-1] // LANES, 2, body)


def block(array_or_shape, width, index):
    shape = getattr(array_or_shape, "shape", array_or_shape)
    return pl.BlockSpec((*shape[:2], width), lambda i: (0, 0, i if index is None else index))


def smooth_inner(own):
    vols, rates, width = own.shape
    outs = [jax.ShapeDtypeStruct((n, vols - EDGE, width), F32) for n in (WIDE, rates - WIDE)]
    wide = width // CHUNKS
    return pl.pallas_call(
        inner_kernel,
        grid=(CHUNKS,),
        out_shape=outs,
        in_specs=[block(own, wide, None)],
        out_specs=[block(o, wide, None) for o in outs],
        compiler_params=pltpu.CompilerParams(vmem_limit_bytes=VMEM_LIMIT),
        cost_estimate=cost(SMOOTH_COST),
        name="smooth_inner",
    )(own)


def smooth_outer(side, own, near, far, chunk):
    _, rates, width = own.shape
    wide = width // CHUNKS
    outs = [jax.ShapeDtypeStruct((n, 2 * EDGE, wide), F32) for n in (WIDE, rates - WIDE)]
    return pl.pallas_call(
        outer_kernel,
        grid=(1,),
        out_shape=outs,
        in_specs=[SMEM] + [block(a, wide, chunk) for a in (own, near, far)],
        out_specs=[block(o, wide, 0) for o in outs],
        compiler_params=pltpu.CompilerParams(vmem_limit_bytes=VMEM_LIMIT),
        cost_estimate=cost(SMOOTH_COST),
        name="smooth_outer",
    )(side, own, near, far)


def settle_kernel(plan, *refs):
    parts, vols, rates, first, last, low, high, k_low, k_high, whole, aliased, waits = plan
    refs = list(refs)
    side = refs.pop(0)
    sources = [refs.pop(0) for _ in range(parts)]
    left_node, left_hi, left_lo, right_hi, right_lo, growth, felicity = [refs.pop(0) for _ in range(7)]
    carried = None if first else (refs.pop(0), refs.pop(0))
    del refs[: aliased + waits]
    outs = [refs.pop(0) for _ in range(1 if whole else 2)]
    handed = None if last else (refs.pop(0), refs.pop(0))
    if whole:
        result = refs.pop(0)
        sem = refs.pop(0)
    windows, turned = refs
    tiles = high - low
    rows = rates * vols
    lane = lax.broadcasted_iota(jnp.int32, (rows, LANES), 1)
    base = 0 if first else 1

    def put(slot, value):
        hi = value.astype(BF16)
        lo = (value - hi.astype(F32)).astype(BF16)
        windows[0:rows, lanes_of(slot)] = hi
        windows[rows:, lanes_of(slot)] = lo

    vol_start, vol_end, at_start, at_end = [side[i] != 0 for i in range(1, 5)]
    if whole:
        edges = [at_start if e < REACH else at_end for e in range(rates + WIDE)]

        def beyond(i, e):
            return e < REACH or e >= rates + REACH

        def layers_of(at):
            return [ref[i, :, at] for ref in sources for i in range(ref.shape[0])]

    else:
        edges = [at_end] * (rates + WIDE)

        def beyond(i, e):
            return (e < rates) != (i < rates - REACH)

        def layers_of(at):
            inner = [ref[i, :, at] for ref in sources[: parts // 2] for i in range(ref.shape[0])]
            outer = [ref[i, :, at] for ref in sources[parts // 2 :] for i in range(ref.shape[0])]
            return [jnp.concatenate([o[:EDGE], n, o[EDGE:]], axis=0) for n, o in zip(inner, outer)]

    if first:
        turned[...] = jnp.zeros_like(turned)
    else:
        windows[:, 0:LANES] = carried[0][...]
        turned[...] = carried[1][...]

    def smooth(tile):
        layers = layers_of(lanes_of(tile))
        kept = [jnp.where(edge, 0.0, layer) for edge, layer in zip(edges, layers)]
        totals = []
        for i in range(rates):
            used = [kept[e] if beyond(i, e) else layers[e] for e in range(i, i + WIDE + 1)]
            total = (SCALE * GAUSS[REACH]) * used[REACH]
            for j in range(REACH):
                total = total + (SCALE * GAUSS[j]) * (used[j] + used[WIDE - j])
            totals.append(total)
        now = pltpu.roll(jnp.concatenate(totals, axis=0), LANES // 2, 1)
        put(tile + base, jnp.where(lane < LANES // 2, turned[...], now))
        turned[...] = now

    repeat(tiles, 4, smooth)
    if last:
        put(tiles + base, jnp.where(lane < LANES // 2, turned[...], 0.0))
    else:
        handed[0][...] = windows[:, lanes_of(tiles + base - 1)]
        handed[1][...] = turned[...]

    depth = lax.broadcasted_iota(jnp.int16, (2 * LANES, LANES), 0)
    nothing = jnp.zeros((2 * LANES, LANES), BF16)
    allocations = left_node.shape[0]

    def choose(tile):
        at = lanes_of(tile + k_low)
        here = lanes_of(tile)
        window = windows[:, lanes_of(tile, 2)]
        total = jnp.zeros((rates, vols, LANES), F32)
        for pair in range(0, allocations, 2):
            his, los = [], []
            for a in (pair, pair + 1):
                node = left_node[a : a + 1, at].astype(jnp.int16)
                is_left = depth == node
                is_right = depth == node + jnp.int16(1)
                his.append(jnp.where(is_left, left_hi[a : a + 1, at], jnp.where(is_right, right_hi[a : a + 1, at], nothing)))
                los.append(jnp.where(is_left, left_lo[a : a + 1, at], jnp.where(is_right, right_lo[a : a + 1, at], nothing)))
            both = jnp.dot(window, jnp.concatenate(his, axis=1), preferred_element_type=F32)
            rest = jnp.dot(window[:rows], jnp.concatenate(los, axis=1), preferred_element_type=F32)
            cont = both[:rows] + both[rows:] + rest
            for q in (0, 1):
                power = jnp.exp2(cont[:, q * LANES : (q + 1) * LANES].reshape(rates, vols, LANES))
                total = total + growth[pair + q] * power
        value = (SMOOTHING * LN2) * jnp.log2(total) + felicity[0:1, at]
        value = jnp.swapaxes(value, 0, 1)
        if whole:
            result[:, :, here] = value
        else:
            half = EDGE // 2
            rows_in = [value[i] for i in range(1, vols - 1)]
            rows_in = (
                [jnp.where(vol_start, 0.0, r) for r in rows_in[: half - 1]]
                + rows_in[half - 1 : 1 - half]
                + [jnp.where(vol_end, 0.0, r) for r in rows_in[1 - half :]]
            )
            onward = jnp.swapaxes(jnp.stack(smooth_rows(rows_in)), 0, 1)
            outs[0][:, :, here] = onward[: rates - WIDE]
            outs[1][:, :, here] = onward[rates - WIDE :]

    repeat(k_high - k_low, 4, choose)
    if whole:
        copy = pltpu.make_async_copy(result, outs[0].at[:, :, pl.ds(k_low * LANES, (k_high - k_low) * LANES)], sem)
        copy.start()
        copy.wait()


def cuts_of(section, index, tiles):
    step = tiles // CHUNKS
    low, high = index * step, (index + 1) * step
    first, last = index == 0, index == CHUNKS - 1
    low, high = (low if first else low - section), (high if last else high - section)
    return low, high, (0 if first else low - 1), (high if last else high - 1)


def settle(side, sources, specs, section, index, tables, growth, carried, out_so_far=None, after=()):
    whole = section == 1
    allocations, wealth = tables[0].shape
    low, high, k_low, k_high = cuts_of(section, index, wealth // LANES)
    first, last = index == 0, index == CHUNKS - 1
    vols = growth.shape[1]
    rates = out_so_far[0] if first and whole else None
    rates = 8 if rates is None else rates
    rows = vols * rates
    count = k_high - k_low
    full = lambda shape: pl.BlockSpec(shape, lambda i: (0,) * len(shape))
    operands = [side, *sources, *tables[:5], growth, tables[5]]
    specs = [SMEM, *specs] + [full(o.shape) for o in operands[1 + len(sources) :]]
    if not first:
        operands += list(carried)
        specs += [full(c.shape) for c in carried]
    aliases = {}
    aliased = whole and not first
    if aliased:
        aliases = {len(operands): 0}
        operands.append(out_so_far)
        specs.append(pl.BlockSpec(memory_space=pl.ANY))
    operands += list(after)
    specs += [pl.BlockSpec(memory_space=pl.ANY)] * len(after)
    scratch = []
    if whole:
        outs = [jax.ShapeDtypeStruct((vols, rates, wealth), F32)]
        out_specs = [pl.BlockSpec(memory_space=pl.ANY)]
        scratch += [pltpu.VMEM((vols, rates, count * LANES), F32), pltpu.SemaphoreType.DMA]
    else:
        outs = [jax.ShapeDtypeStruct((n, vols - EDGE, count * LANES), F32) for n in (rates - WIDE, WIDE)]
        out_specs = [full(o.shape) for o in outs]
    cut = len(outs)
    if not last:
        more = [jax.ShapeDtypeStruct((2 * rows, LANES), BF16), jax.ShapeDtypeStruct((rows, LANES), F32)]
        outs += more
        out_specs += [full(o.shape) for o in more]
    slots = (high - low) + (0 if first else 1) + (1 if last else 0)
    scratch += [pltpu.VMEM((2 * rows, slots * LANES), BF16), pltpu.VMEM((rows, LANES), F32)]
    plan = (len(sources), vols, rates, first, last, low, high, k_low, k_high, whole, aliased, len(after))
    got = pl.pallas_call(
        functools.partial(settle_kernel, plan),
        grid=(1,),
        out_shape=outs,
        in_specs=specs,
        out_specs=out_specs,
        scratch_shapes=scratch,
        input_output_aliases=aliases,
        compiler_params=pltpu.CompilerParams(vmem_limit_bytes=VMEM_LIMIT),
        cost_estimate=cost(SETTLE_COST),
        name="settle",
    )(*operands)
    return got[:cut], got[cut:]


def parts_of(x):
    hi = lax.reduce_precision(x, 8, 7)
    return hi.astype(BF16), (x - hi).astype(BF16)


def on_device(value_next, risk_cost, band_start, band_weight, felicity_array):
    vols, rates, wealth = value_next.shape
    vol_count, rate_count = lax.axis_size("vol"), lax.axis_size("rate")
    vol_at, rate_at = lax.axis_index("vol"), lax.axis_index("rate")
    paired = [(i, i ^ 1) for i in range(vol_count)]
    across = [(i, ((i + 1) ^ 1) - 1) for i in range(1, vol_count - 1)]
    rate_back = [(i, (i - 1) % rate_count) for i in range(rate_count)]
    rate_on = [(i, (i + 1) % rate_count) for i in range(rate_count)]

    core = vol_at % 2
    flags = [core == 0, vol_at == 0, vol_at == vol_count - 1, rate_at == 0, rate_at == rate_count - 1]
    side = jnp.stack(flags).astype(jnp.int32)

    risk_rows = jnp.pad(risk_cost.T[:, :, None], ((0, 0), (0, 0), (0, LANES - 1)))
    near_at = jnp.where(core == 0, vols - WIDE, 0)
    near, far = [
        jnp.concatenate([lax.dynamic_slice_in_dim(a, at, WIDE, axis=0) for a in (value_next, risk_rows)], axis=2)
        for at in (near_at, vols - WIDE - near_at)
    ]
    far = lax.ppermute(far, "vol", across)
    near = lax.ppermute(near, "vol", paired)

    inner = smooth_inner(value_next)
    inner = (*inner, lax.ppermute(inner[0], "rate", rate_back))
    outer = [smooth_outer(side, value_next, near, far, c) for c in range(CHUNKS)]
    outer = [(*o, lax.ppermute(o[0], "rate", rate_back)) for o in outer]

    window_start = (lax.broadcasted_iota(jnp.int32, band_start.shape, 1) // LANES) * LANES - LANES // 2
    tables = (band_start - window_start, *parts_of(1.0 - band_weight), *parts_of(band_weight), felicity_array[None, :])
    near_risk, far_risk = [a[:, :, wealth].T for a in (near, far)]
    low_risk = jnp.where(core == 0, far_risk, near_risk)[:, WIDE - EDGE // 2 :]
    high_risk = jnp.where(core == 0, near_risk, far_risk)[:, : EDGE // 2]
    growth_here, growth_wide = [
        jnp.broadcast_to(jnp.exp(r * (-1.0 / SMOOTHING))[:, :, None], (*r.shape, LANES))
        for r in (risk_cost, jnp.concatenate([low_risk, risk_cost, high_risk], axis=1))
    ]

    wide = wealth // CHUNKS
    onward, carried = [], None
    for c in range(CHUNKS):
        sources = (*inner, *outer[c])
        specs = [block(a, wide, c) for a in inner] + [block(a, wide, 0) for a in outer[c]]
        pieces, carried = settle(side, sources, specs, 0, c, tables, growth_wide, carried)
        onward.append((lax.ppermute(pieces[1], "rate", rate_on), *pieces))

    out, carried = (rates,), None
    for c in range(CHUNKS):
        specs = [block(a, a.shape[2], 0) for a in onward[c]]
        (out,), carried = settle(side, onward[c], specs, 1, c, tables, growth_here, carried, out)
    return out


def solution(mesh):
    return jax.shard_map(
        on_device,
        mesh=mesh,
        in_specs=(P("vol", "rate", None), P(None, "vol"), P(), P(), P()),
        out_specs=P("vol", "rate", None),
        check_vma=False,
    )
```

```python
import functools

import jax
import jax.numpy as jnp
from jax import lax
from jax.experimental import pallas as pl
from jax.experimental.pallas import tpu as pltpu
from jax.sharding import PartitionSpec as P

GAUSS = (
    0.000548269,
    0.030757124,
    0.240123178,
    0.457142857,
    0.240123178,
    0.030757124,
    0.000548269,
)
REACH = 3
WIDE = 2 * REACH
LOG2E = 1.4426950408889634
LN2 = 0.6931471805599453
DISCOUNT = 0.96
SMOOTHING = 0.5
LANES = 128
SCALE = DISCOUNT / SMOOTHING * LOG2E

F32 = jnp.float32
BF16 = jnp.bfloat16

CHUNKS = 4
EDGE = 8
SMOOTH_COST = 10**9
SETTLE_COST = 4 * 10**9

SMEM = pl.BlockSpec(memory_space=pltpu.SMEM)
VMEM = pl.BlockSpec(memory_space=pltpu.VMEM)
VMEM_LIMIT = 10 * 2**20


def repeat(count, step, body):
    turns = count // step
    if turns > 1:

        def turn(t, carry):
            for q in range(step):
                body(t * step + q)
            return carry

        lax.fori_loop(0, turns, turn, 0)
        done = turns * step
    else:
        done = 0
    for q in range(done, count):
        body(q)


def lanes_of(tile, count=1):
    if isinstance(tile, int):
        return pl.ds(tile * LANES, count * LANES)
    return pl.ds(pl.multiple_of(tile * LANES, LANES), count * LANES)


def cost(flops):
    return pl.CostEstimate(flops=flops, bytes_accessed=0, transcendentals=0)


def smooth_rows(layers):
    rows = []
    for i in range(len(layers) - WIDE):
        total = GAUSS[REACH] * layers[i + REACH]
        for j in range(REACH):
            total = total + GAUSS[j] * (layers[i + j] + layers[i + WIDE - j])
        rows.append(total)
    return rows


def inner_kernel(own, sent, kept):
    def body(tile):
        at = lanes_of(tile)
        first = EDGE // 2
        layers = [own[i, :, at] for i in range(first - REACH, own.shape[0] - first + REACH)]
        turned = jnp.swapaxes(jnp.stack(smooth_rows(layers)), 0, 1)
        sent[:, :, at] = turned[:WIDE]
        kept[:, :, at] = turned[WIDE:]

    repeat(own.shape[-1] // LANES, 2, body)


def outer_kernel(side, own, near, far, sent, kept):
    first_core = side[0] != 0

    def body(tile):
        at = lanes_of(tile)
        pairs = [(near[i, :, at], far[i, :, at]) for i in range(WIDE)]
        low = [jnp.where(first_core, f, n) for n, f in pairs]
        high = [jnp.where(first_core, n, f) for n, f in pairs]
        count = own.shape[0]
        half = EDGE // 2
        low += [own[i, :, at] for i in range(half + REACH)]
        high = [own[i, :, at] for i in range(count - half - REACH, count)] + high
        nothing = jnp.zeros_like(low[0])
        rows = [nothing] + smooth_rows(low) + smooth_rows(high) + [nothing]
        turned = jnp.swapaxes(jnp.stack(rows), 0, 1)
        sent[:, :, at] = turned[:WIDE]
        kept[:, :, at] = turned[WIDE:]

    repeat(own.shape[-1] // LANES, 2, body)


def block(array_or_shape, width, index):
    shape = getattr(array_or_shape, "shape", array_or_shape)
    return pl.BlockSpec((*shape[:2], width), lambda i: (0, 0, i if index is None else index))


def smooth_inner(own):
    vols, rates, width = own.shape
    outs = [jax.ShapeDtypeStruct((n, vols - EDGE, width), F32) for n in (WIDE, rates - WIDE)]
    wide = width // CHUNKS
    return pl.pallas_call(
        inner_kernel,
        grid=(CHUNKS,),
        out_shape=outs,
        in_specs=[block(own, wide, None)],
        out_specs=[block(o, wide, None) for o in outs],
        compiler_params=pltpu.CompilerParams(vmem_limit_bytes=VMEM_LIMIT),
        cost_estimate=cost(SMOOTH_COST),
        name="smooth_inner",
    )(own)


def smooth_outer(side, own, near, far, chunk):
    _, rates, width = own.shape
    wide = width // CHUNKS
    outs = [jax.ShapeDtypeStruct((n, 2 * EDGE, wide), F32) for n in (WIDE, rates - WIDE)]
    return pl.pallas_call(
        outer_kernel,
        grid=(1,),
        out_shape=outs,
        in_specs=[SMEM] + [block(a, wide, chunk) for a in (own, near, far)],
        out_specs=[block(o, wide, 0) for o in outs],
        compiler_params=pltpu.CompilerParams(vmem_limit_bytes=VMEM_LIMIT),
        cost_estimate=cost(SMOOTH_COST),
        name="smooth_outer",
    )(side, own, near, far)


def settle_kernel(plan, *refs):
    parts, vols, rates, first, last, low, high, k_low, k_high, whole, aliased, waits = plan
    refs = list(refs)
    side = refs.pop(0)
    sources = [refs.pop(0) for _ in range(parts)]
    left_node, left_hi, left_lo, right_hi, right_lo, growth, felicity = [refs.pop(0) for _ in range(7)]
    carried = None if first else (refs.pop(0), refs.pop(0))
    del refs[: aliased + waits]
    outs = [refs.pop(0) for _ in range(1 if whole else 2)]
    handed = None if last else (refs.pop(0), refs.pop(0))
    if whole:
        result = refs.pop(0)
        sem = refs.pop(0)
    windows, turned = refs
    tiles = high - low
    rows = rates * vols
    lane = lax.broadcasted_iota(jnp.int32, (rows, LANES), 1)
    base = 0 if first else 1

    def put(slot, value):
        hi = value.astype(BF16)
        lo = (value - hi.astype(F32)).astype(BF16)
        windows[0:rows, lanes_of(slot)] = hi
        windows[rows:, lanes_of(slot)] = lo

    vol_start, vol_end, at_start, at_end = [side[i] != 0 for i in range(1, 5)]
    if whole:
        edges = [at_start if e < REACH else at_end for e in range(rates + WIDE)]

        def beyond(i, e):
            return e < REACH or e >= rates + REACH

        def layers_of(at):
            return [ref[i, :, at] for ref in sources for i in range(ref.shape[0])]

    else:
        edges = [at_end] * (rates + WIDE)

        def beyond(i, e):
            return (e < rates) != (i < rates - REACH)

        def layers_of(at):
            inner = [ref[i, :, at] for ref in sources[: parts // 2] for i in range(ref.shape[0])]
            outer = [ref[i, :, at] for ref in sources[parts // 2 :] for i in range(ref.shape[0])]
            return [jnp.concatenate([o[:EDGE], n, o[EDGE:]], axis=0) for n, o in zip(inner, outer)]

    if first:
        turned[...] = jnp.zeros_like(turned)
    else:
        windows[:, 0:LANES] = carried[0][...]
        turned[...] = carried[1][...]

    def smooth(tile):
        layers = layers_of(lanes_of(tile))
        kept = [jnp.where(edge, 0.0, layer) for edge, layer in zip(edges, layers)]
        totals = []
        for i in range(rates):
            used = [kept[e] if beyond(i, e) else layers[e] for e in range(i, i + WIDE + 1)]
            total = (SCALE * GAUSS[REACH]) * used[REACH]
            for j in range(REACH):
                total = total + (SCALE * GAUSS[j]) * (used[j] + used[WIDE - j])
            totals.append(total)
        now = pltpu.roll(jnp.concatenate(totals, axis=0), LANES // 2, 1)
        put(tile + base, jnp.where(lane < LANES // 2, turned[...], now))
        turned[...] = now

    repeat(tiles, 4, smooth)
    if last:
        put(tiles + base, jnp.where(lane < LANES // 2, turned[...], 0.0))
    else:
        handed[0][...] = windows[:, lanes_of(tiles + base - 1)]
        handed[1][...] = turned[...]

    depth = lax.broadcasted_iota(jnp.int16, (2 * LANES, LANES), 0)
    nothing = jnp.zeros((2 * LANES, LANES), BF16)
    allocations = left_node.shape[0]

    def choose(tile):
        at = lanes_of(tile + k_low)
        here = lanes_of(tile)
        window = windows[:, lanes_of(tile, 2)]
        total = jnp.zeros((rates, vols, LANES), F32)
        for pair in range(0, allocations, 2):
            his, los = [], []
            for a in (pair, pair + 1):
                node = left_node[a : a + 1, at].astype(jnp.int16)
                is_left = depth == node
                is_right = depth == node + jnp.int16(1)
                his.append(jnp.where(is_left, left_hi[a : a + 1, at], jnp.where(is_right, right_hi[a : a + 1, at], nothing)))
                los.append(jnp.where(is_left, left_lo[a : a + 1, at], jnp.where(is_right, right_lo[a : a + 1, at], nothing)))
            both = jnp.dot(window, jnp.concatenate(his, axis=1), preferred_element_type=F32)
            rest = jnp.dot(window[:rows], jnp.concatenate(los, axis=1), preferred_element_type=F32)
            cont = both[:rows] + both[rows:] + rest
            for q in (0, 1):
                power = jnp.exp2(cont[:, q * LANES : (q + 1) * LANES].reshape(rates, vols, LANES))
                total = total + growth[pair + q] * power
        value = (SMOOTHING * LN2) * jnp.log2(total) + felicity[0:1, at]
        value = jnp.swapaxes(value, 0, 1)
        if whole:
            result[:, :, here] = value
        else:
            half = EDGE // 2
            rows_in = [value[i] for i in range(1, vols - 1)]
            rows_in = (
                [jnp.where(vol_start, 0.0, r) for r in rows_in[: half - 1]]
                + rows_in[half - 1 : 1 - half]
                + [jnp.where(vol_end, 0.0, r) for r in rows_in[1 - half :]]
            )
            onward = jnp.swapaxes(jnp.stack(smooth_rows(rows_in)), 0, 1)
            outs[0][:, :, here] = onward[: rates - WIDE]
            outs[1][:, :, here] = onward[rates - WIDE :]

    repeat(k_high - k_low, 4, choose)
    if whole:
        copy = pltpu.make_async_copy(result, outs[0].at[:, :, pl.ds(k_low * LANES, (k_high - k_low) * LANES)], sem)
        copy.start()
        copy.wait()


def cuts_of(section, index, tiles):
    step = tiles // CHUNKS
    low, high = index * step, (index + 1) * step
    first, last = index == 0, index == CHUNKS - 1
    low, high = (low if first else low - section), (high if last else high - section)
    return low, high, (0 if first else low - 1), (high if last else high - 1)


def settle(side, sources, specs, section, index, tables, growth, carried, out_so_far=None, after=()):
    whole = section == 1
    allocations, wealth = tables[0].shape
    low, high, k_low, k_high = cuts_of(section, index, wealth // LANES)
    first, last = index == 0, index == CHUNKS - 1
    vols = growth.shape[1]
    rates = out_so_far[0] if first and whole else None
    rates = 8 if rates is None else rates
    rows = vols * rates
    count = k_high - k_low
    full = lambda shape: pl.BlockSpec(shape, lambda i: (0,) * len(shape))
    operands = [side, *sources, *tables[:5], growth, tables[5]]
    specs = [SMEM, *specs] + [full(o.shape) for o in operands[1 + len(sources) :]]
    if not first:
        operands += list(carried)
        specs += [full(c.shape) for c in carried]
    aliases = {}
    aliased = whole and not first
    if aliased:
        aliases = {len(operands): 0}
        operands.append(out_so_far)
        specs.append(pl.BlockSpec(memory_space=pl.ANY))
    operands += list(after)
    specs += [pl.BlockSpec(memory_space=pl.ANY)] * len(after)
    scratch = []
    if whole:
        outs = [jax.ShapeDtypeStruct((vols, rates, wealth), F32)]
        out_specs = [pl.BlockSpec(memory_space=pl.ANY)]
        scratch += [pltpu.VMEM((vols, rates, count * LANES), F32), pltpu.SemaphoreType.DMA]
    else:
        outs = [jax.ShapeDtypeStruct((n, vols - EDGE, count * LANES), F32) for n in (rates - WIDE, WIDE)]
        out_specs = [full(o.shape) for o in outs]
    cut = len(outs)
    if not last:
        more = [jax.ShapeDtypeStruct((2 * rows, LANES), BF16), jax.ShapeDtypeStruct((rows, LANES), F32)]
        outs += more
        out_specs += [full(o.shape) for o in more]
    slots = (high - low) + (0 if first else 1) + (1 if last else 0)
    scratch += [pltpu.VMEM((2 * rows, slots * LANES), BF16), pltpu.VMEM((rows, LANES), F32)]
    plan = (len(sources), vols, rates, first, last, low, high, k_low, k_high, whole, aliased, len(after))
    got = pl.pallas_call(
        functools.partial(settle_kernel, plan),
        grid=(1,),
        out_shape=outs,
        in_specs=specs,
        out_specs=out_specs,
        scratch_shapes=scratch,
        input_output_aliases=aliases,
        compiler_params=pltpu.CompilerParams(vmem_limit_bytes=VMEM_LIMIT),
        cost_estimate=cost(SETTLE_COST),
        name="settle",
    )(*operands)
    return got[:cut], got[cut:]


def parts_of(x):
    hi = lax.reduce_precision(x, 8, 7)
    return hi.astype(BF16), (x - hi).astype(BF16)


def on_device(value_next, risk_cost, band_start, band_weight, felicity_array):
    vols, rates, wealth = value_next.shape
    vol_count, rate_count = lax.axis_size("vol"), lax.axis_size("rate")
    vol_at, rate_at = lax.axis_index("vol"), lax.axis_index("rate")
    paired = [(i, i ^ 1) for i in range(vol_count)]
    across = [(i, ((i + 1) ^ 1) - 1) for i in range(1, vol_count - 1)]
    rate_back = [(i, (i - 1) % rate_count) for i in range(rate_count)]
    rate_on = [(i, (i + 1) % rate_count) for i in range(rate_count)]

    core = vol_at % 2
    flags = [core == 0, vol_at == 0, vol_at == vol_count - 1, rate_at == 0, rate_at == rate_count - 1]
    side = jnp.stack(flags).astype(jnp.int32)

    risk_rows = jnp.pad(risk_cost.T[:, :, None], ((0, 0), (0, 0), (0, LANES - 1)))
    near_at = jnp.where(core == 0, vols - WIDE, 0)
    near, far = [
        jnp.concatenate([lax.dynamic_slice_in_dim(a, at, WIDE, axis=0) for a in (value_next, risk_rows)], axis=2)
        for at in (near_at, vols - WIDE - near_at)
    ]
    far = lax.ppermute(far, "vol", across)
    near = lax.ppermute(near, "vol", paired)

    inner = smooth_inner(value_next)
    inner = (*inner, lax.ppermute(inner[0], "rate", rate_back))
    outer = [smooth_outer(side, value_next, near, far, c) for c in range(CHUNKS)]
    outer = [(*o, lax.ppermute(o[0], "rate", rate_back)) for o in outer]

    window_start = (lax.broadcasted_iota(jnp.int32, band_start.shape, 1) // LANES) * LANES - LANES // 2
    tables = (band_start - window_start, *parts_of(1.0 - band_weight), *parts_of(band_weight), felicity_array[None, :])
    near_risk, far_risk = [a[:, :, wealth].T for a in (near, far)]
    low_risk = jnp.where(core == 0, far_risk, near_risk)[:, WIDE - EDGE // 2 :]
    high_risk = jnp.where(core == 0, near_risk, far_risk)[:, : EDGE // 2]
    growth_here, growth_wide = [
        jnp.broadcast_to(jnp.exp(r * (-1.0 / SMOOTHING))[:, :, None], (*r.shape, LANES))
        for r in (risk_cost, jnp.concatenate([low_risk, risk_cost, high_risk], axis=1))
    ]

    wide = wealth // CHUNKS
    onward, carried = [], None
    for c in range(CHUNKS):
        sources = (*inner, *outer[c])
        specs = [block(a, wide, c) for a in inner] + [block(a, wide, 0) for a in outer[c]]
        pieces, carried = settle(side, sources, specs, 0, c, tables, growth_wide, carried)
        onward.append((lax.ppermute(pieces[1], "rate", rate_on), *pieces))

    out, carried = (rates,), None
    for c in range(CHUNKS):
        specs = [block(a, a.shape[2], 0) for a in onward[c]]
        (out,), carried = settle(side, onward[c], specs, 1, c, tables, growth_here, carried, out)
    return out


def solution(mesh):
    return jax.shard_map(
        on_device,
        mesh=mesh,
        in_specs=(P("vol", "rate", None), P(None, "vol"), P(), P(), P()),
        out_specs=P("vol", "rate", None),
        check_vma=False,
    )
```

```python
import functools

import jax
import jax.numpy as jnp
from jax import lax
from jax.experimental import pallas as pl
from jax.experimental.pallas import tpu as pltpu
from jax.sharding import PartitionSpec as P

GAUSS = (
    0.000548269,
    0.030757124,
    0.240123178,
    0.457142857,
    0.240123178,
    0.030757124,
    0.000548269,
)
REACH = 3
WIDE = 2 * REACH
LOG2E = 1.4426950408889634
LN2 = 0.6931471805599453
DISCOUNT = 0.96
SMOOTHING = 0.5
LANES = 128
SCALE = DISCOUNT / SMOOTHING * LOG2E

F32 = jnp.float32
BF16 = jnp.bfloat16

CHUNKS = 4
EDGE = 8
SMOOTH_COST = 10**9
SETTLE_COST = 4 * 10**9

SMEM = pl.BlockSpec(memory_space=pltpu.SMEM)
VMEM = pl.BlockSpec(memory_space=pltpu.VMEM)
VMEM_LIMIT = 10 * 2**20


def repeat(count, step, body):
    turns = count // step
    if turns > 1:

        def turn(t, carry):
            for q in range(step):
                body(t * step + q)
            return carry

        lax.fori_loop(0, turns, turn, 0)
        done = turns * step
    else:
        done = 0
    for q in range(done, count):
        body(q)


def lanes_of(tile, count=1):
    if isinstance(tile, int):
        return pl.ds(tile * LANES, count * LANES)
    return pl.ds(pl.multiple_of(tile * LANES, LANES), count * LANES)


def cost(flops):
    return pl.CostEstimate(flops=flops, bytes_accessed=0, transcendentals=0)


def smooth_rows(layers):
    rows = []
    for i in range(len(layers) - WIDE):
        total = GAUSS[REACH] * layers[i + REACH]
        for j in range(REACH):
            total = total + GAUSS[j] * (layers[i + j] + layers[i + WIDE - j])
        rows.append(total)
    return rows


def inner_kernel(own, sent, kept):
    def body(tile):
        at = lanes_of(tile)
        first = EDGE // 2
        layers = [own[i, :, at] for i in range(first - REACH, own.shape[0] - first + REACH)]
        turned = jnp.swapaxes(jnp.stack(smooth_rows(layers)), 0, 1)
        sent[:, :, at] = turned[:WIDE]
        kept[:, :, at] = turned[WIDE:]

    repeat(own.shape[-1] // LANES, 4, body)


def outer_kernel(side, own, near, far, sent, kept):
    first_core = side[0] != 0

    def body(tile):
        at = lanes_of(tile)
        pairs = [(near[i, :, at], far[i, :, at]) for i in range(WIDE)]
        low = [jnp.where(first_core, f, n) for n, f in pairs]
        high = [jnp.where(first_core, n, f) for n, f in pairs]
        count = own.shape[0]
        half = EDGE // 2
        low += [own[i, :, at] for i in range(half + REACH)]
        high = [own[i, :, at] for i in range(count - half - REACH, count)] + high
        nothing = jnp.zeros_like(low[0])
        rows = [nothing] + smooth_rows(low) + smooth_rows(high) + [nothing]
        turned = jnp.swapaxes(jnp.stack(rows), 0, 1)
        sent[:, :, at] = turned[:WIDE]
        kept[:, :, at] = turned[WIDE:]

    repeat(own.shape[-1] // LANES, 4, body)


def block(array_or_shape, width, index):
    shape = getattr(array_or_shape, "shape", array_or_shape)
    return pl.BlockSpec((*shape[:2], width), lambda i: (0, 0, i if index is None else index))


def smooth_inner(own):
    vols, rates, width = own.shape
    outs = [jax.ShapeDtypeStruct((n, vols - EDGE, width), F32) for n in (WIDE, rates - WIDE)]
    wide = width // CHUNKS
    return pl.pallas_call(
        inner_kernel,
        grid=(CHUNKS,),
        out_shape=outs,
        in_specs=[block(own, wide, None)],
        out_specs=[block(o, wide, None) for o in outs],
        compiler_params=pltpu.CompilerParams(vmem_limit_bytes=VMEM_LIMIT),
        cost_estimate=cost(SMOOTH_COST),
        name="smooth_inner",
    )(own)


def smooth_outer(side, own, near, far, chunk):
    _, rates, width = own.shape
    wide = width // CHUNKS
    outs = [jax.ShapeDtypeStruct((n, 2 * EDGE, wide), F32) for n in (WIDE, rates - WIDE)]
    return pl.pallas_call(
        outer_kernel,
        grid=(1,),
        out_shape=outs,
        in_specs=[SMEM] + [block(a, wide, chunk) for a in (own, near, far)],
        out_specs=[block(o, wide, 0) for o in outs],
        compiler_params=pltpu.CompilerParams(vmem_limit_bytes=VMEM_LIMIT),
        cost_estimate=cost(SMOOTH_COST),
        name="smooth_outer",
    )(side, own, near, far)


def settle_kernel(plan, *refs):
    parts, vols, rates, first, last, low, high, k_low, k_high, whole, aliased, waits = plan
    refs = list(refs)
    side = refs.pop(0)
    sources = [refs.pop(0) for _ in range(parts)]
    left_node, left_hi, left_lo, right_hi, right_lo, growth, felicity = [refs.pop(0) for _ in range(7)]
    carried = None if first else (refs.pop(0), refs.pop(0))
    del refs[: aliased + waits]
    outs = [refs.pop(0) for _ in range(1 if whole else 2)]
    handed = None if last else (refs.pop(0), refs.pop(0))
    if whole:
        result = refs.pop(0)
        sem = refs.pop(0)
    windows, turned = refs
    tiles = high - low
    rows = rates * vols
    lane = lax.broadcasted_iota(jnp.int32, (rows, LANES), 1)
    base = 0 if first else 1

    def put(slot, value):
        hi = value.astype(BF16)
        lo = (value - hi.astype(F32)).astype(BF16)
        windows[0:rows, lanes_of(slot)] = hi
        windows[rows:, lanes_of(slot)] = lo

    vol_start, vol_end, at_start, at_end = [side[i] != 0 for i in range(1, 5)]
    if whole:
        edges = [at_start if e < REACH else at_end for e in range(rates + WIDE)]

        def beyond(i, e):
            return e < REACH or e >= rates + REACH

        def layers_of(at):
            return [ref[i, :, at] for ref in sources for i in range(ref.shape[0])]

    else:
        edges = [at_end] * (rates + WIDE)

        def beyond(i, e):
            return (e < rates) != (i < rates - REACH)

        def layers_of(at):
            inner = [ref[i, :, at] for ref in sources[: parts // 2] for i in range(ref.shape[0])]
            outer = [ref[i, :, at] for ref in sources[parts // 2 :] for i in range(ref.shape[0])]
            return [jnp.concatenate([o[:EDGE], n, o[EDGE:]], axis=0) for n, o in zip(inner, outer)]

    if first:
        turned[...] = jnp.zeros_like(turned)
    else:
        windows[:, 0:LANES] = carried[0][...]
        turned[...] = carried[1][...]

    def smooth(tile):
        layers = layers_of(lanes_of(tile))
        kept = [jnp.where(edge, 0.0, layer) for edge, layer in zip(edges, layers)]
        totals = []
        for i in range(rates):
            used = [kept[e] if beyond(i, e) else layers[e] for e in range(i, i + WIDE + 1)]
            total = (SCALE * GAUSS[REACH]) * used[REACH]
            for j in range(REACH):
                total = total + (SCALE * GAUSS[j]) * (used[j] + used[WIDE - j])
            totals.append(total)
        now = pltpu.roll(jnp.concatenate(totals, axis=0), LANES // 2, 1)
        put(tile + base, jnp.where(lane < LANES // 2, turned[...], now))
        turned[...] = now

    repeat(tiles, 4, smooth)
    if last:
        put(tiles + base, jnp.where(lane < LANES // 2, turned[...], 0.0))
    else:
        handed[0][...] = windows[:, lanes_of(tiles + base - 1)]
        handed[1][...] = turned[...]

    depth = lax.broadcasted_iota(jnp.int16, (2 * LANES, LANES), 0)
    nothing = jnp.zeros((2 * LANES, LANES), BF16)
    allocations = left_node.shape[0]

    def choose(tile):
        at = lanes_of(tile + k_low)
        here = lanes_of(tile)
        window = windows[:, lanes_of(tile, 2)]
        total = jnp.zeros((rates, vols, LANES), F32)
        for pair in range(0, allocations, 2):
            his, los = [], []
            for a in (pair, pair + 1):
                node = left_node[a : a + 1, at].astype(jnp.int16)
                is_left = depth == node
                is_right = depth == node + jnp.int16(1)
                his.append(jnp.where(is_left, left_hi[a : a + 1, at], jnp.where(is_right, right_hi[a : a + 1, at], nothing)))
                los.append(jnp.where(is_left, left_lo[a : a + 1, at], jnp.where(is_right, right_lo[a : a + 1, at], nothing)))
            both = jnp.dot(window, jnp.concatenate(his, axis=1), preferred_element_type=F32)
            rest = jnp.dot(window[:rows], jnp.concatenate(los, axis=1), preferred_element_type=F32)
            cont = both[:rows] + both[rows:] + rest
            for q in (0, 1):
                power = jnp.exp2(cont[:, q * LANES : (q + 1) * LANES].reshape(rates, vols, LANES))
                total = total + growth[pair + q] * power
        value = (SMOOTHING * LN2) * jnp.log2(total) + felicity[0:1, at]
        value = jnp.swapaxes(value, 0, 1)
        if whole:
            result[:, :, here] = value
        else:
            half = EDGE // 2
            rows_in = [value[i] for i in range(1, vols - 1)]
            rows_in = (
                [jnp.where(vol_start, 0.0, r) for r in rows_in[: half - 1]]
                + rows_in[half - 1 : 1 - half]
                + [jnp.where(vol_end, 0.0, r) for r in rows_in[1 - half :]]
            )
            onward = jnp.swapaxes(jnp.stack(smooth_rows(rows_in)), 0, 1)
            outs[0][:, :, here] = onward[: rates - WIDE]
            outs[1][:, :, here] = onward[rates - WIDE :]

    repeat(k_high - k_low, 4, choose)
    if whole:
        copy = pltpu.make_async_copy(result, outs[0].at[:, :, pl.ds(k_low * LANES, (k_high - k_low) * LANES)], sem)
        copy.start()
        copy.wait()


def cuts_of(section, index, tiles):
    step = tiles // CHUNKS
    low, high = index * step, (index + 1) * step
    first, last = index == 0, index == CHUNKS - 1
    low, high = (low if first else low - section), (high if last else high - section)
    return low, high, (0 if first else low - 1), (high if last else high - 1)


def settle(side, sources, specs, section, index, tables, growth, carried, out_so_far=None, after=()):
    whole = section == 1
    allocations, wealth = tables[0].shape
    low, high, k_low, k_high = cuts_of(section, index, wealth // LANES)
    first, last = index == 0, index == CHUNKS - 1
    vols = growth.shape[1]
    rates = out_so_far[0] if first and whole else None
    rates = 8 if rates is None else rates
    rows = vols * rates
    count = k_high - k_low
    full = lambda shape: pl.BlockSpec(shape, lambda i: (0,) * len(shape))
    operands = [side, *sources, *tables[:5], growth, tables[5]]
    specs = [SMEM, *specs] + [full(o.shape) for o in operands[1 + len(sources) :]]
    if not first:
        operands += list(carried)
        specs += [full(c.shape) for c in carried]
    aliases = {}
    aliased = whole and not first
    if aliased:
        aliases = {len(operands): 0}
        operands.append(out_so_far)
        specs.append(pl.BlockSpec(memory_space=pl.ANY))
    operands += list(after)
    specs += [pl.BlockSpec(memory_space=pl.ANY)] * len(after)
    scratch = []
    if whole:
        outs = [jax.ShapeDtypeStruct((vols, rates, wealth), F32)]
        out_specs = [pl.BlockSpec(memory_space=pl.ANY)]
        scratch += [pltpu.VMEM((vols, rates, count * LANES), F32), pltpu.SemaphoreType.DMA]
    else:
        outs = [jax.ShapeDtypeStruct((n, vols - EDGE, count * LANES), F32) for n in (rates - WIDE, WIDE)]
        out_specs = [full(o.shape) for o in outs]
    cut = len(outs)
    if not last:
        more = [jax.ShapeDtypeStruct((2 * rows, LANES), BF16), jax.ShapeDtypeStruct((rows, LANES), F32)]
        outs += more
        out_specs += [full(o.shape) for o in more]
    slots = (high - low) + (0 if first else 1) + (1 if last else 0)
    scratch += [pltpu.VMEM((2 * rows, slots * LANES), BF16), pltpu.VMEM((rows, LANES), F32)]
    plan = (len(sources), vols, rates, first, last, low, high, k_low, k_high, whole, aliased, len(after))
    got = pl.pallas_call(
        functools.partial(settle_kernel, plan),
        grid=(1,),
        out_shape=outs,
        in_specs=specs,
        out_specs=out_specs,
        scratch_shapes=scratch,
        input_output_aliases=aliases,
        compiler_params=pltpu.CompilerParams(vmem_limit_bytes=VMEM_LIMIT),
        cost_estimate=cost(SETTLE_COST),
        name="settle",
    )(*operands)
    return got[:cut], got[cut:]


def parts_of(x):
    hi = lax.reduce_precision(x, 8, 7)
    return hi.astype(BF16), (x - hi).astype(BF16)


def on_device(value_next, risk_cost, band_start, band_weight, felicity_array):
    vols, rates, wealth = value_next.shape
    vol_count, rate_count = lax.axis_size("vol"), lax.axis_size("rate")
    vol_at, rate_at = lax.axis_index("vol"), lax.axis_index("rate")
    paired = [(i, i ^ 1) for i in range(vol_count)]
    across = [(i, ((i + 1) ^ 1) - 1) for i in range(1, vol_count - 1)]
    rate_back = [(i, (i - 1) % rate_count) for i in range(rate_count)]
    rate_on = [(i, (i + 1) % rate_count) for i in range(rate_count)]

    core = vol_at % 2
    flags = [core == 0, vol_at == 0, vol_at == vol_count - 1, rate_at == 0, rate_at == rate_count - 1]
    side = jnp.stack(flags).astype(jnp.int32)

    risk_rows = jnp.pad(risk_cost.T[:, :, None], ((0, 0), (0, 0), (0, LANES - 1)))
    near_at = jnp.where(core == 0, vols - WIDE, 0)
    near, far = [
        jnp.concatenate([lax.dynamic_slice_in_dim(a, at, WIDE, axis=0) for a in (value_next, risk_rows)], axis=2)
        for at in (near_at, vols - WIDE - near_at)
    ]
    far = lax.ppermute(far, "vol", across)
    near = lax.ppermute(near, "vol", paired)

    inner = smooth_inner(value_next)
    inner = (*inner, lax.ppermute(inner[0], "rate", rate_back))
    outer = [smooth_outer(side, value_next, near, far, c) for c in range(CHUNKS)]
    outer = [(*o, lax.ppermute(o[0], "rate", rate_back)) for o in outer]

    window_start = (lax.broadcasted_iota(jnp.int32, band_start.shape, 1) // LANES) * LANES - LANES // 2
    tables = (band_start - window_start, *parts_of(1.0 - band_weight), *parts_of(band_weight), felicity_array[None, :])
    near_risk, far_risk = [a[:, :, wealth].T for a in (near, far)]
    low_risk = jnp.where(core == 0, far_risk, near_risk)[:, WIDE - EDGE // 2 :]
    high_risk = jnp.where(core == 0, near_risk, far_risk)[:, : EDGE // 2]
    growth_here, growth_wide = [
        jnp.broadcast_to(jnp.exp(r * (-1.0 / SMOOTHING))[:, :, None], (*r.shape, LANES))
        for r in (risk_cost, jnp.concatenate([low_risk, risk_cost, high_risk], axis=1))
    ]

    wide = wealth // CHUNKS
    onward, carried = [], None
    for c in range(CHUNKS):
        sources = (*inner, *outer[c])
        specs = [block(a, wide, c) for a in inner] + [block(a, wide, 0) for a in outer[c]]
        pieces, carried = settle(side, sources, specs, 0, c, tables, growth_wide, carried)
        onward.append((lax.ppermute(pieces[1], "rate", rate_on), *pieces))

    out, carried = (rates,), None
    for c in range(CHUNKS):
        specs = [block(a, a.shape[2], 0) for a in onward[c]]
        (out,), carried = settle(side, onward[c], specs, 1, c, tables, growth_here, carried, out)
    return out


def solution(mesh):
    return jax.shard_map(
        on_device,
        mesh=mesh,
        in_specs=(P("vol", "rate", None), P(None, "vol"), P(), P(), P()),
        out_specs=P("vol", "rate", None),
        check_vma=False,
    )
```

```python
import functools

import jax
import jax.numpy as jnp
from jax import lax
from jax.experimental import pallas as pl
from jax.experimental.pallas import tpu as pltpu
from jax.sharding import PartitionSpec as P

GAUSS = (
    0.000548269,
    0.030757124,
    0.240123178,
    0.457142857,
    0.240123178,
    0.030757124,
    0.000548269,
)
REACH = 3
WIDE = 2 * REACH
LOG2E = 1.4426950408889634
LN2 = 0.6931471805599453
DISCOUNT = 0.96
SMOOTHING = 0.5
LANES = 128
SCALE = DISCOUNT / SMOOTHING * LOG2E

F32 = jnp.float32
BF16 = jnp.bfloat16

CHUNKS = 4
EDGE = 8
SMOOTH_COST = 10**9
SETTLE_COST = 4 * 10**9

SMEM = pl.BlockSpec(memory_space=pltpu.SMEM)
VMEM = pl.BlockSpec(memory_space=pltpu.VMEM)
VMEM_LIMIT = 10 * 2**20


def repeat(count, step, body):
    turns = count // step
    if turns > 1:

        def turn(t, carry):
            for q in range(step):
                body(t * step + q)
            return carry

        lax.fori_loop(0, turns, turn, 0)
        done = turns * step
    else:
        done = 0
    for q in range(done, count):
        body(q)


def lanes_of(tile, count=1):
    if isinstance(tile, int):
        return pl.ds(tile * LANES, count * LANES)
    return pl.ds(pl.multiple_of(tile * LANES, LANES), count * LANES)


def cost(flops):
    return pl.CostEstimate(flops=flops, bytes_accessed=0, transcendentals=0)


def smooth_rows(layers):
    rows = []
    for i in range(len(layers) - WIDE):
        total = GAUSS[REACH] * layers[i + REACH]
        for j in range(REACH):
            total = total + GAUSS[j] * (layers[i + j] + layers[i + WIDE - j])
        rows.append(total)
    return rows


def inner_kernel(own, sent, kept):
    def body(tile):
        at = lanes_of(tile)
        first = EDGE // 2
        layers = [own[i, :, at] for i in range(first - REACH, own.shape[0] - first + REACH)]
        turned = jnp.swapaxes(jnp.stack(smooth_rows(layers)), 0, 1)
        sent[:, :, at] = turned[:WIDE]
        kept[:, :, at] = turned[WIDE:]

    repeat(own.shape[-1] // LANES, 4, body)


def outer_kernel(side, own, near, far, sent, kept):
    first_core = side[0] != 0

    def body(tile):
        at = lanes_of(tile)
        pairs = [(near[i, :, at], far[i, :, at]) for i in range(WIDE)]
        low = [jnp.where(first_core, f, n) for n, f in pairs]
        high = [jnp.where(first_core, n, f) for n, f in pairs]
        count = own.shape[0]
        half = EDGE // 2
        low += [own[i, :, at] for i in range(half + REACH)]
        high = [own[i, :, at] for i in range(count - half - REACH, count)] + high
        nothing = jnp.zeros_like(low[0])
        rows = [nothing] + smooth_rows(low) + smooth_rows(high) + [nothing]
        turned = jnp.swapaxes(jnp.stack(rows), 0, 1)
        sent[:, :, at] = turned[:WIDE]
        kept[:, :, at] = turned[WIDE:]

    repeat(own.shape[-1] // LANES, 4, body)


def block(array_or_shape, width, index):
    shape = getattr(array_or_shape, "shape", array_or_shape)
    return pl.BlockSpec((*shape[:2], width), lambda i: (0, 0, i if index is None else index))


def smooth_inner(own):
    vols, rates, width = own.shape
    outs = [jax.ShapeDtypeStruct((n, vols - EDGE, width), F32) for n in (WIDE, rates - WIDE)]
    wide = width // CHUNKS
    return pl.pallas_call(
        inner_kernel,
        grid=(CHUNKS,),
        out_shape=outs,
        in_specs=[block(own, wide, None)],
        out_specs=[block(o, wide, None) for o in outs],
        compiler_params=pltpu.CompilerParams(vmem_limit_bytes=VMEM_LIMIT),
        cost_estimate=cost(SMOOTH_COST),
        name="smooth_inner",
    )(own)


def smooth_outer(side, own, near, far, chunk):
    _, rates, width = own.shape
    wide = width // CHUNKS
    outs = [jax.ShapeDtypeStruct((n, 2 * EDGE, wide), F32) for n in (WIDE, rates - WIDE)]
    return pl.pallas_call(
        outer_kernel,
        grid=(1,),
        out_shape=outs,
        in_specs=[SMEM] + [block(a, wide, chunk) for a in (own, near, far)],
        out_specs=[block(o, wide, 0) for o in outs],
        compiler_params=pltpu.CompilerParams(vmem_limit_bytes=VMEM_LIMIT),
        cost_estimate=cost(SMOOTH_COST),
        name="smooth_outer",
    )(side, own, near, far)


def settle_kernel(plan, *refs):
    parts, vols, rates, first, last, low, high, k_low, k_high, whole, aliased, waits = plan
    refs = list(refs)
    side = refs.pop(0)
    sources = [refs.pop(0) for _ in range(parts)]
    left_node, left_hi, left_lo, right_hi, right_lo, growth, felicity = [refs.pop(0) for _ in range(7)]
    carried = None if first else (refs.pop(0), refs.pop(0))
    del refs[: aliased + waits]
    outs = [refs.pop(0) for _ in range(1 if whole else 2)]
    handed = None if last else (refs.pop(0), refs.pop(0))
    if whole:
        result = refs.pop(0)
        sem = refs.pop(0)
    windows, turned = refs
    tiles = high - low
    rows = rates * vols
    lane = lax.broadcasted_iota(jnp.int32, (rows, LANES), 1)
    base = 0 if first else 1

    def put(slot, value):
        hi = value.astype(BF16)
        lo = (value - hi.astype(F32)).astype(BF16)
        windows[0:rows, lanes_of(slot)] = hi
        windows[rows:, lanes_of(slot)] = lo

    vol_start, vol_end, at_start, at_end = [side[i] != 0 for i in range(1, 5)]
    if whole:
        edges = [at_start if e < REACH else at_end for e in range(rates + WIDE)]

        def beyond(i, e):
            return e < REACH or e >= rates + REACH

        def layers_of(at):
            return [ref[i, :, at] for ref in sources for i in range(ref.shape[0])]

    else:
        edges = [at_end] * (rates + WIDE)

        def beyond(i, e):
            return (e < rates) != (i < rates - REACH)

        def layers_of(at):
            inner = [ref[i, :, at] for ref in sources[: parts // 2] for i in range(ref.shape[0])]
            outer = [ref[i, :, at] for ref in sources[parts // 2 :] for i in range(ref.shape[0])]
            return [jnp.concatenate([o[:EDGE], n, o[EDGE:]], axis=0) for n, o in zip(inner, outer)]

    if first:
        turned[...] = jnp.zeros_like(turned)
    else:
        windows[:, 0:LANES] = carried[0][...]
        turned[...] = carried[1][...]

    def smooth(tile):
        layers = layers_of(lanes_of(tile))
        kept = [jnp.where(edge, 0.0, layer) for edge, layer in zip(edges, layers)]
        totals = []
        for i in range(rates):
            used = [kept[e] if beyond(i, e) else layers[e] for e in range(i, i + WIDE + 1)]
            total = (SCALE * GAUSS[REACH]) * used[REACH]
            for j in range(REACH):
                total = total + (SCALE * GAUSS[j]) * (used[j] + used[WIDE - j])
            totals.append(total)
        now = pltpu.roll(jnp.concatenate(totals, axis=0), LANES // 2, 1)
        put(tile + base, jnp.where(lane < LANES // 2, turned[...], now))
        turned[...] = now

    repeat(tiles, 4, smooth)
    if last:
        put(tiles + base, jnp.where(lane < LANES // 2, turned[...], 0.0))
    else:
        handed[0][...] = windows[:, lanes_of(tiles + base - 1)]
        handed[1][...] = turned[...]

    depth = lax.broadcasted_iota(jnp.int16, (2 * LANES, LANES), 0)
    nothing = jnp.zeros((2 * LANES, LANES), BF16)
    allocations = left_node.shape[0]

    def choose(tile):
        at = lanes_of(tile + k_low)
        here = lanes_of(tile)
        window = windows[:, lanes_of(tile, 2)]
        total = jnp.zeros((rates, vols, LANES), F32)
        for pair in range(0, allocations, 2):
            his, los = [], []
            for a in (pair, pair + 1):
                node = left_node[a : a + 1, at].astype(jnp.int16)
                is_left = depth == node
                is_right = depth == node + jnp.int16(1)
                his.append(jnp.where(is_left, left_hi[a : a + 1, at], jnp.where(is_right, right_hi[a : a + 1, at], nothing)))
                los.append(jnp.where(is_left, left_lo[a : a + 1, at], jnp.where(is_right, right_lo[a : a + 1, at], nothing)))
            both = jnp.dot(window, jnp.concatenate(his, axis=1), preferred_element_type=F32)
            rest = jnp.dot(window[:rows], jnp.concatenate(los, axis=1), preferred_element_type=F32)
            cont = both[:rows] + both[rows:] + rest
            for q in (0, 1):
                power = jnp.exp2(cont[:, q * LANES : (q + 1) * LANES].reshape(rates, vols, LANES))
                total = total + growth[pair + q] * power
        value = (SMOOTHING * LN2) * jnp.log2(total) + felicity[0:1, at]
        value = jnp.swapaxes(value, 0, 1)
        if whole:
            result[:, :, here] = value
        else:
            half = EDGE // 2
            rows_in = [value[i] for i in range(1, vols - 1)]
            rows_in = (
                [jnp.where(vol_start, 0.0, r) for r in rows_in[: half - 1]]
                + rows_in[half - 1 : 1 - half]
                + [jnp.where(vol_end, 0.0, r) for r in rows_in[1 - half :]]
            )
            onward = jnp.swapaxes(jnp.stack(smooth_rows(rows_in)), 0, 1)
            outs[0][:, :, here] = onward[: rates - WIDE]
            outs[1][:, :, here] = onward[rates - WIDE :]

    count = k_high - k_low
    half = count // 2 if whole else count
    repeat(half, 4, choose)
    if whole:

        def give(begin, length, which):
            to = outs[0].at[:, :, pl.ds((k_low + begin) * LANES, length * LANES)]
            return pltpu.make_async_copy(result.at[:, :, pl.ds(begin * LANES, length * LANES)], to, sem.at[which])

        early, late = give(0, half, 0), give(half, count - half, 1)
        early.start()
        repeat(count - half, 4, lambda tile: choose(tile + half))
        late.start()
        early.wait()
        late.wait()


def cuts_of(section, index, tiles):
    step = tiles // CHUNKS
    low, high = index * step, (index + 1) * step
    first, last = index == 0, index == CHUNKS - 1
    low, high = (low if first else low - section), (high if last else high - section)
    return low, high, (0 if first else low - 1), (high if last else high - 1)


def settle(side, sources, specs, section, index, tables, growth, carried, out_so_far=None, after=()):
    whole = section == 1
    allocations, wealth = tables[0].shape
    low, high, k_low, k_high = cuts_of(section, index, wealth // LANES)
    first, last = index == 0, index == CHUNKS - 1
    vols = growth.shape[1]
    rates = out_so_far[0] if first and whole else None
    rates = 8 if rates is None else rates
    rows = vols * rates
    count = k_high - k_low
    full = lambda shape: pl.BlockSpec(shape, lambda i: (0,) * len(shape))
    operands = [side, *sources, *tables[:5], growth, tables[5]]
    specs = [SMEM, *specs] + [full(o.shape) for o in operands[1 + len(sources) :]]
    if not first:
        operands += list(carried)
        specs += [full(c.shape) for c in carried]
    aliases = {}
    aliased = whole and not first
    if aliased:
        aliases = {len(operands): 0}
        operands.append(out_so_far)
        specs.append(pl.BlockSpec(memory_space=pl.ANY))
    operands += list(after)
    specs += [pl.BlockSpec(memory_space=pl.ANY)] * len(after)
    scratch = []
    if whole:
        outs = [jax.ShapeDtypeStruct((vols, rates, wealth), F32)]
        out_specs = [pl.BlockSpec(memory_space=pl.ANY)]
        scratch += [pltpu.VMEM((vols, rates, count * LANES), F32), pltpu.SemaphoreType.DMA((2,))]
    else:
        outs = [jax.ShapeDtypeStruct((n, vols - EDGE, count * LANES), F32) for n in (rates - WIDE, WIDE)]
        out_specs = [full(o.shape) for o in outs]
    cut = len(outs)
    if not last:
        more = [jax.ShapeDtypeStruct((2 * rows, LANES), BF16), jax.ShapeDtypeStruct((rows, LANES), F32)]
        outs += more
        out_specs += [full(o.shape) for o in more]
    slots = (high - low) + (0 if first else 1) + (1 if last else 0)
    scratch += [pltpu.VMEM((2 * rows, slots * LANES), BF16), pltpu.VMEM((rows, LANES), F32)]
    plan = (len(sources), vols, rates, first, last, low, high, k_low, k_high, whole, aliased, len(after))
    got = pl.pallas_call(
        functools.partial(settle_kernel, plan),
        grid=(1,),
        out_shape=outs,
        in_specs=specs,
        out_specs=out_specs,
        scratch_shapes=scratch,
        input_output_aliases=aliases,
        compiler_params=pltpu.CompilerParams(vmem_limit_bytes=VMEM_LIMIT),
        cost_estimate=cost(SETTLE_COST),
        name="settle",
    )(*operands)
    return got[:cut], got[cut:]


def parts_of(x):
    hi = lax.reduce_precision(x, 8, 7)
    return hi.astype(BF16), (x - hi).astype(BF16)


def on_device(value_next, risk_cost, band_start, band_weight, felicity_array):
    vols, rates, wealth = value_next.shape
    vol_count, rate_count = lax.axis_size("vol"), lax.axis_size("rate")
    vol_at, rate_at = lax.axis_index("vol"), lax.axis_index("rate")
    paired = [(i, i ^ 1) for i in range(vol_count)]
    across = [(i, ((i + 1) ^ 1) - 1) for i in range(1, vol_count - 1)]
    rate_back = [(i, (i - 1) % rate_count) for i in range(rate_count)]
    rate_on = [(i, (i + 1) % rate_count) for i in range(rate_count)]

    core = vol_at % 2
    flags = [core == 0, vol_at == 0, vol_at == vol_count - 1, rate_at == 0, rate_at == rate_count - 1]
    side = jnp.stack(flags).astype(jnp.int32)

    risk_rows = jnp.pad(risk_cost.T[:, :, None], ((0, 0), (0, 0), (0, LANES - 1)))
    near_at = jnp.where(core == 0, vols - WIDE, 0)
    near, far = [
        jnp.concatenate([lax.dynamic_slice_in_dim(a, at, WIDE, axis=0) for a in (value_next, risk_rows)], axis=2)
        for at in (near_at, vols - WIDE - near_at)
    ]
    far = lax.ppermute(far, "vol", across)
    near = lax.ppermute(near, "vol", paired)

    inner = smooth_inner(value_next)
    inner = (*inner, lax.ppermute(inner[0], "rate", rate_back))
    outer = [smooth_outer(side, value_next, near, far, c) for c in range(CHUNKS)]
    outer = [(*o, lax.ppermute(o[0], "rate", rate_back)) for o in outer]

    window_start = (lax.broadcasted_iota(jnp.int32, band_start.shape, 1) // LANES) * LANES - LANES // 2
    tables = (band_start - window_start, *parts_of(1.0 - band_weight), *parts_of(band_weight), felicity_array[None, :])
    near_risk, far_risk = [a[:, :, wealth].T for a in (near, far)]
    low_risk = jnp.where(core == 0, far_risk, near_risk)[:, WIDE - EDGE // 2 :]
    high_risk = jnp.where(core == 0, near_risk, far_risk)[:, : EDGE // 2]
    growth_here, growth_wide = [
        jnp.broadcast_to(jnp.exp(r * (-1.0 / SMOOTHING))[:, :, None], (*r.shape, LANES))
        for r in (risk_cost, jnp.concatenate([low_risk, risk_cost, high_risk], axis=1))
    ]

    wide = wealth // CHUNKS
    onward, carried = [], None
    for c in range(CHUNKS):
        sources = (*inner, *outer[c])
        specs = [block(a, wide, c) for a in inner] + [block(a, wide, 0) for a in outer[c]]
        pieces, carried = settle(side, sources, specs, 0, c, tables, growth_wide, carried)
        onward.append((lax.ppermute(pieces[1], "rate", rate_on), *pieces))

    out, carried = (rates,), None
    for c in range(CHUNKS):
        specs = [block(a, a.shape[2], 0) for a in onward[c]]
        (out,), carried = settle(side, onward[c], specs, 1, c, tables, growth_here, carried, out)
    return out


def solution(mesh):
    return jax.shard_map(
        on_device,
        mesh=mesh,
        in_specs=(P("vol", "rate", None), P(None, "vol"), P(), P(), P()),
        out_specs=P("vol", "rate", None),
        check_vma=False,
    )
```
